32 devices in a mesh: grp: 2 (over y), date: 4 (over z), row: 4 (over x, core).
Axes of the slice: x: 2, y: 2, z: 4, core: 2. Of those that a mesh axis runs over, the one named last changes fastest.
Arguments:
- stack_data: float32 [16, 2, 64, 512], P(('grp', 'date'), None, 'row'), parts along dimension 0, may hold values from -40 to 40, as said below
- plan: int32 [8], replicated, may hold values from 0 to 7, each once
Outputs:
- coherence: float32 [16, 8, 2, 64, 512], P(('grp', 'date'), None, None, 'row'), parts along dimension 0
The draws below stay inside these ranges and needn't reach their ends.
There are 2 independent parts, one for each index of `grp`. The reference program is written for one: setup_inputs(seed, part) draws one part's arguments, and reference() takes and returns one part's arrays. A program takes and returns all parts, laid end to end along the dimension named above; an argument that names none is the same for every part. Nothing has to cross between parts.
Inputs may be any that keep to these rules, and one draw needn't show every extreme that they name: `stack_data`: complex samples of one scene seen on every date, each date with its own phase, strength and noise.
All inputs are finite; a program needn't handle non-finite values.
Results may differ from the reference program's by a relative error of at most 0.00005.
Values sent between devices are 32-bit elements; how exact they have to be, the bound alone decides.
No kernel may reach another device: no remote copies, remote signals or barrier semaphores. Data moves between devices by JAX's collectives and lax.ppermute only.
A program may use at most 64 MiB of HBM per device.

```python
import jax
import jax.numpy as jnp
from jax import lax

COLS = 512
HALF_ROWS = 4
HALF_COLS = 16
DATES = 8
ROWS = 64


def draw_stack_data(key, part):
    keys = jax.random.split(jax.random.fold_in(key, 17), 5)
    scene = jax.random.normal(keys[0], (2, ROWS, COLS), jnp.float32)
    phase = jax.random.uniform(keys[1], (DATES, 1, 1), jnp.float32, -3.14159, 3.14159)
    strength = jax.random.uniform(keys[2], (DATES, 1, 1), jnp.float32, 0.3, 1.5)
    noise_level = jnp.exp(jax.random.uniform(keys[3], (DATES, 1, 1, 1), jnp.float32, jnp.log(0.3), jnp.log(2.0)))
    noise = jax.random.normal(keys[4], (DATES, 2, ROWS, COLS), jnp.float32)
    turned_real = jnp.cos(phase) * scene[0][None] - jnp.sin(phase) * scene[1][None]
    turned_imag = jnp.sin(phase) * scene[0][None] + jnp.cos(phase) * scene[1][None]
    signal = strength[:, None] * jnp.stack([turned_real, turned_imag], axis=1)
    values = signal + noise_level * noise
    return jnp.clip(values, -40.0, 40.0)


def setup_inputs(seed: int = 0, part: int = 0) -> dict:
    arg_keys = jax.random.split(jax.random.key(seed), 3)
    part_keys = jax.random.split(jax.random.fold_in(arg_keys[2], part), 3)
    stack_data = draw_stack_data(jax.random.fold_in(jax.random.fold_in(arg_keys[2], part), 71), part)
    plan = jax.random.permutation(arg_keys[1], DATES).astype(jnp.int32)
    return {"stack_data": stack_data, "plan": plan}


def window_sum(field):
    lead = [(0, 0)] * (field.ndim - 2)
    padded = jnp.pad(field, lead + [(HALF_ROWS + 1, HALF_ROWS), (HALF_COLS + 1, HALF_COLS)])
    rowsum = jnp.cumsum(padded, axis=-2)
    rowsum = rowsum[..., 2 * HALF_ROWS + 1:, :] - rowsum[..., :ROWS, :]
    colsum = jnp.cumsum(rowsum, axis=-1)
    return colsum[..., 2 * HALF_COLS + 1:] - colsum[..., :COLS]

def reference(stack_data, plan):
    real_part = stack_data[:, 0]
    imag_part = stack_data[:, 1]
    power = window_sum(real_part * real_part + imag_part * imag_part)
    order_real = real_part[plan]
    order_imag = imag_part[plan]
    order_power = power[plan]

    def one_date(which):
        base_real = real_part[which]
        base_imag = imag_part[which]
        cross_real = window_sum(base_real[None] * order_real + base_imag[None] * order_imag)
        cross_imag = window_sum(base_imag[None] * order_real - base_real[None] * order_imag)
        factor = 1.0 / jnp.sqrt(power[which][None] * order_power + 1e-06)
        return jnp.stack([cross_real * factor, cross_imag * factor], axis=1)
    return lax.map(one_date, jnp.arange(DATES, dtype=jnp.int32))
```

```python
import functools

import jax
import jax.numpy as jnp
from jax import lax
from jax.experimental import pallas as pl
from jax.experimental.pallas import tpu as pltpu
from jax.sharding import PartitionSpec as P

HALF_ROWS = 4
HALF_COLS = 16
epsilon = 1e-06


def split(x):
    high = x.astype(jnp.bfloat16)
    low = (x - high.astype(jnp.float32)).astype(jnp.bfloat16)
    return high, low


def row_window(f, rows):
    length = f.shape[0]
    total, width = f, 1
    while width < 2 * HALF_ROWS:
        total = total + pltpu.roll(total, length - width, 0)
        width *= 2
    return total[:rows] + f[2 * HALF_ROWS:]


def kernel(n_parts, nd, direct, plan_ref, own_ref, own_a, own_b, *rest):
    parts = rest[:n_parts]
    rim_a = rest[n_parts:2 * n_parts]
    rim_b = rest[2 * n_parts:3 * n_parts]
    band_ref, out_ref, ext, res, buf, where, sems = rest[3 * n_parts:]
    rows, cols = own_ref.shape[2], own_ref.shape[3]
    per_part = parts[0].shape[0]
    slots = n_parts * per_part
    n_dates = plan_ref.shape[0]
    me = lax.axis_index("date")
    odd = lax.axis_index("row") % 2 == 1
    step = pl.program_id(0)

    def place(k, _):
        j = plan_ref[k]
        if direct:
            slot = ((j // nd) ^ me) * nd + j % nd
        else:
            slot = j
        where[slot] = k
        return 0

    @pl.when(step == 0)
    def _():
        lax.fori_loop(0, n_dates, place, 0)

    def fill(dst, block, ra, rb):
        a, b = ra[...], rb[...]
        ext[dst, :, :HALF_ROWS] = jnp.where(odd, a, b)
        ext[dst, :, HALF_ROWS:HALF_ROWS + rows] = block[...]
        ext[dst, :, HALF_ROWS + rows:] = jnp.where(odd, b, a)

    band = band_ref[...]

    def columns(fields):
        high, low = zip(*(split(f) for f in fields))
        both = jnp.concatenate(high + low, axis=0)
        out = jnp.dot(both, band, preferred_element_type=jnp.float32)
        half = out.shape[0] // 2
        return out[:half] + out[half:]

    mine = slice(slots, slots + nd)
    for d in range(nd):
        fill(slots + d, own_ref.at[d], own_a.at[d], own_b.at[d])
    for p in range(n_parts):
        for d in range(per_part):
            fill(p * per_part + d, parts[p].at[d], rim_a[p].at[d], rim_b[p].at[d])

    own_fields = []
    for d in range(nd):
        re, im = ext[slots + d, 0], ext[slots + d, 1]
        own_fields.append(row_window(re * re + im * im, rows))
    own_power = columns(own_fields)
    copies = []
    for s in range(slots):
        re, im = ext[s, 0], ext[s, 1]
        fields = [row_window(re * re + im * im, rows)]
        for d in range(nd):
            mr, mi = ext[slots + d, 0], ext[slots + d, 1]
            fields.append(row_window(mr * re + mi * im, rows))
            fields.append(row_window(mi * re - mr * im, rows))
        res[s] = columns(fields)
        power = res[s, :rows]
        k = where[step * slots + s]
        for d in range(nd):
            factor = lax.rsqrt(own_power[d * rows:(d + 1) * rows] * power + epsilon)
            at = (1 + 2 * d) * rows
            buf[s, d, 0] = res[s, at:at + rows] * factor
            buf[s, d, 1] = res[s, at + rows:at + 2 * rows] * factor
            copy = pltpu.make_async_copy(buf.at[s, d], out_ref.at[d, k], sems.at[s, d])
            copy.start()
            copies.append(copy)
    for copy in copies:
        copy.wait()


def pairs_of(size, flip):
    return [(i, i ^ flip) for i in range(size) if (i ^ flip) < size]


def body(stack_data, plan):
    nd, _, rows, cols = stack_data.shape
    size, n_rows = lax.axis_size("date"), lax.axis_size("row")
    direct = size in (2, 4)
    odd = lax.axis_index("row") % 2

    inner = pairs_of(n_rows, 1)
    outer = [(i, i + 1) for i in range(1, n_rows - 1, 2)]
    outer = outer + [(j, i) for i, j in outer]

    def rims(blocks):
        last = [b[:, :, rows - HALF_ROWS:] for b in blocks]
        first = [b[:, :, :HALF_ROWS] for b in blocks]
        last, first = (jnp.concatenate(x, axis=0) for x in (last, first))
        a = lax.ppermute(jnp.where(odd == 1, first, last), "row", inner)
        b = lax.ppermute(jnp.where(odd == 1, last, first), "row", outer)
        return a, b

    if direct:
        parts = [stack_data] + [
            lax.ppermute(stack_data, "date", pairs_of(size, m)) for m in range(1, size)
        ]
        a, b = rims(parts)
        n_parts, per_part, grid = size, nd, 1
        rim_a = [a[m * nd:(m + 1) * nd] for m in range(size)]
        rim_b = [b[m * nd:(m + 1) * nd] for m in range(size)]
        own_a, own_b = rim_a[0], rim_b[0]
    else:
        gathered = lax.all_gather(stack_data, "date", axis=0, tiled=True)
        a, b = rims([gathered, stack_data])
        n_parts, per_part = 1, 8 if (size * nd) % 8 == 0 else nd
        grid = size * nd // per_part
        parts, rim_a, rim_b = [gathered], [a[:size * nd]], [b[:size * nd]]
        own_a, own_b = a[size * nd:], b[size * nd:]

    out_col = lax.broadcasted_iota(jnp.int32, (cols, cols), 0)
    in_col = lax.broadcasted_iota(jnp.int32, (cols, cols), 1)
    band = (jnp.abs(out_col - in_col) <= HALF_COLS).astype(jnp.bfloat16)

    slots = n_parts * per_part

    def whole(shape):
        return pl.BlockSpec(shape, lambda g: (0,) * len(shape))

    def chunk(shape):
        return pl.BlockSpec(shape, lambda g: (g, 0, 0, 0))

    rim_shape = (HALF_ROWS, cols)
    return pl.pallas_call(
        functools.partial(kernel, n_parts, nd, direct),
        grid=(grid,),
        out_shape=jax.ShapeDtypeStruct((nd, size * nd, 2, rows, cols), jnp.float32),
        in_specs=[
            pl.BlockSpec(memory_space=pltpu.SMEM),
            whole((nd, 2, rows, cols)),
            whole((nd, 2) + rim_shape),
            whole((nd, 2) + rim_shape),
        ]
        + [chunk((per_part, 2, rows, cols))] * n_parts
        + [chunk((per_part, 2) + rim_shape)] * (2 * n_parts)
        + [whole((cols, cols))],
        out_specs=pl.BlockSpec(memory_space=pl.ANY),
        scratch_shapes=[
            pltpu.VMEM((slots + nd, 2, rows + 2 * HALF_ROWS, cols), jnp.float32),
            pltpu.VMEM((slots, (1 + 2 * nd) * rows, cols), jnp.float32),
            pltpu.VMEM((slots, nd, 2, rows, cols), jnp.float32),
            pltpu.SMEM((size * nd,), jnp.int32),
            pltpu.SemaphoreType.DMA((slots, nd)),
        ],
        compiler_params=pltpu.CompilerParams(vmem_limit_bytes=32 * 2**20),
        name="coherence",
    )(plan, stack_data, own_a, own_b, *parts, *rim_a, *rim_b, band)


def solution(mesh):
    placed = (P(("grp", "date"), None, "row", None), P())
    return jax.shard_map(
        body,
        mesh=mesh,
        in_specs=placed,
        out_specs=P(("grp", "date"), None, None, "row", None),
        check_vma=False,
    )
```

```python
import functools

import jax
import jax.numpy as jnp
from jax import lax
from jax.experimental import pallas as pl
from jax.experimental.pallas import tpu as pltpu
from jax.sharding import PartitionSpec as P

HALF_ROWS = 4
HALF_COLS = 16
epsilon = 1e-06


def split(x):
    high = x.astype(jnp.bfloat16)
    low = (x - high.astype(jnp.float32)).astype(jnp.bfloat16)
    return high, low


def row_window(f, rows):
    length = f.shape[0]
    total, width = f, 1
    while width < 2 * HALF_ROWS:
        total = total + pltpu.roll(total, length - width, 0)
        width *= 2
    return total[:rows] + f[2 * HALF_ROWS:]


def kernel(counts, nd, direct, n_rows, plan_ref, *refs):
    n_blocks, n_rims = len(counts[0]), len(counts[1])
    edges, refs = refs[:n_blocks], refs[n_blocks:]
    inners, refs = refs[:n_blocks], refs[n_blocks:]
    rim_c, refs = refs[:n_rims], refs[n_rims:]
    rim_x, refs = refs[:n_rims], refs[n_rims:]
    band_ref, out_ref, ext, res, buf, where, sems = refs
    half = HALF_ROWS
    rows, cols = inners[0].shape[2] + 2 * half, inners[0].shape[3]
    total = sum(counts[0])
    first = 0 if direct else nd
    slots = total - first
    row = lax.axis_index("row")
    me = lax.axis_index("date")
    odd = row % 2 == 1
    step = 0 if direct else pl.program_id(0)

    def place(k, _):
        j = plan_ref[k]
        where[((j // nd) ^ me) * nd + j % nd if direct else j] = k
        return 0

    if direct:
        lax.fori_loop(0, plan_ref.shape[0], place, 0)
    else:

        @pl.when(step == 0)
        def _():
            lax.fori_loop(0, plan_ref.shape[0], place, 0)

    at = 0
    for ref, inner, count in zip(edges, inners, counts[0]):
        for d in range(count):
            ext[at, :, half:2 * half] = ref[d, :, half:]
            ext[at, :, 2 * half:rows] = inner[d]
            ext[at, :, rows:rows + half] = ref[d, :, :half]
            at += 1
    at = 0
    for c, x, count in zip(rim_c, rim_x, counts[1]):
        for d in range(count):
            top = jnp.where(odd, c[d], x[d])
            bottom = jnp.where(odd, x[d], c[d])
            ext[at, :, :half] = jnp.where(row == 0, 0.0, top)
            ext[at, :, rows + half:] = jnp.where(row == n_rows - 1, 0.0, bottom)
            at += 1

    band = band_ref[...]

    def columns(fields):
        high, low = zip(*(split(f) for f in fields))
        both = jnp.concatenate(high + low, axis=0)
        out = jnp.dot(both, band, preferred_element_type=jnp.float32)
        middle = out.shape[0] // 2
        return out[:middle] + out[middle:]

    own_fields = []
    for d in range(nd):
        re, im = ext[d, 0], ext[d, 1]
        own_fields.append(row_window(re * re + im * im, rows))
    own_power = columns(own_fields)
    copies = []
    for s in range(slots):
        re, im = ext[first + s, 0], ext[first + s, 1]
        fields = [row_window(re * re + im * im, rows)]
        for d in range(nd):
            mr, mi = ext[d, 0], ext[d, 1]
            fields.append(row_window(mr * re + mi * im, rows))
            fields.append(row_window(mi * re - mr * im, rows))
        res[s] = columns(fields)
        power = res[s, :rows]
        k = where[step * slots + s]
        for d in range(nd):
            factor = lax.rsqrt(own_power[d * rows:(d + 1) * rows] * power + epsilon)
            at = (1 + 2 * d) * rows
            buf[s, d, 0] = res[s, at:at + rows] * factor
            buf[s, d, 1] = res[s, at + rows:at + 2 * rows] * factor
            copy = pltpu.make_async_copy(buf.at[s, d], out_ref.at[d, k], sems.at[s, d])
            copy.start()
            copies.append(copy)
    for copy in copies:
        copy.wait()


def pairs_of(size, flip):
    return [(i, i ^ flip) for i in range(size)]


def body(stack_data, plan):
    nd, _, rows, cols = stack_data.shape
    size, n_rows = lax.axis_size("date"), lax.axis_size("row")
    half = HALF_ROWS
    direct = size == 4
    odd = lax.axis_index("row") % 2 == 1

    near = [(i, i ^ 1) for i in range(n_rows) if (i ^ 1) < n_rows]
    far = [(i, (i + 1) % n_rows) for i in range(1, n_rows, 2)] if n_rows % 2 == 0 else [
        (i, i + 1) for i in range(1, n_rows - 1, 2)]
    far = far + [(j, i) for i, j in far if i != j]

    def cut(block):
        first, last = block[:, :, :half], block[:, :, rows - half:]
        return jnp.concatenate([last, first], axis=2), block[:, :, half:rows - half]

    def rims(edge):
        last, first = edge[:, :, :half], edge[:, :, half:]
        c = lax.ppermute(jnp.where(odd, first, last), "row", near)
        x = lax.ppermute(jnp.where(odd, last, first), "row", far)
        return c, x

    edge, inner = cut(stack_data)
    if direct:
        edge_2 = lax.ppermute(edge, "date", pairs_of(size, 2))
        edge_1 = lax.ppermute(edge, "date", pairs_of(size, 1))
        inner_2 = lax.ppermute(inner, "date", pairs_of(size, 2))
        inner_1 = lax.ppermute(inner, "date", pairs_of(size, 1))
        edge_3 = lax.ppermute(edge_2, "date", pairs_of(size, 1))
        rims_a = rims(jnp.concatenate([edge, edge_1, edge_2], axis=0))
        inner_3 = lax.ppermute(inner_2, "date", pairs_of(size, 1))
        rims_b = rims(edge_3)
        edges, inners = [edge, edge_1, edge_2, edge_3], [inner, inner_1, inner_2, inner_3]
        rim_c, rim_x = [rims_a[0], rims_b[0]], [rims_a[1], rims_b[1]]
        chunked = [False] * 4, [False] * 2
        grid, slots = None, size * nd
    else:
        gathered = lax.all_gather(stack_data, "date", axis=0, tiled=True)
        all_edge, all_inner = cut(gathered)
        rim_own, rim_all = rims(edge), rims(all_edge)
        edges, inners = [edge, all_edge], [inner, all_inner]
        rim_c, rim_x = [rim_own[0], rim_all[0]], [rim_own[1], rim_all[1]]
        chunked = [False, True], [False, True]
        slots = 8 if (size * nd) % 8 == 0 else nd
        grid = (size * nd // slots,)

    out_col = lax.broadcasted_iota(jnp.int32, (cols, cols), 0)
    in_col = lax.broadcasted_iota(jnp.int32, (cols, cols), 1)
    band = (jnp.abs(out_col - in_col) <= HALF_COLS).astype(jnp.bfloat16)

    def spec(array, chunk=False):
        if grid is None:
            return pl.BlockSpec(memory_space=pltpu.VMEM)
        if chunk:
            return pl.BlockSpec((slots,) + array.shape[1:], lambda g: (g, 0, 0, 0))
        return pl.BlockSpec(array.shape, lambda g: (0,) * array.ndim)

    def count(arrays, chunks):
        return [slots if c else a.shape[0] for a, c in zip(arrays, chunks)]

    counts = count(edges, chunked[0]), count(rim_c, chunked[1])
    total = sum(counts[0])
    operands = edges + inners + rim_c + rim_x
    chunks = chunked[0] * 2 + chunked[1] * 2
    return pl.pallas_call(
        functools.partial(kernel, counts, nd, direct, n_rows),
        **({} if grid is None else {"grid": grid}),
        out_shape=jax.ShapeDtypeStruct((nd, size * nd, 2, rows, cols), jnp.float32),
        in_specs=[pl.BlockSpec(memory_space=pltpu.SMEM)]
        + [spec(a, c) for a, c in zip(operands, chunks)]
        + [spec(band)],
        out_specs=pl.BlockSpec(memory_space=pl.ANY),
        scratch_shapes=[
            pltpu.VMEM((total, 2, rows + 2 * half, cols), jnp.float32),
            pltpu.VMEM((slots, (1 + 2 * nd) * rows, cols), jnp.float32),
            pltpu.VMEM((slots, nd, 2, rows, cols), jnp.float32),
            pltpu.SMEM((size * nd,), jnp.int32),
            pltpu.SemaphoreType.DMA((slots, nd)),
        ],
        compiler_params=pltpu.CompilerParams(vmem_limit_bytes=32 * 2**20),
        name="coherence",
    )(plan, *operands, band)


def solution(mesh):
    placed = (P(("grp", "date"), None, "row", None), P())
    return jax.shard_map(
        body,
        mesh=mesh,
        in_specs=placed,
        out_specs=P(("grp", "date"), None, None, "row", None),
        check_vma=False,
    )
```

```python
import functools

import jax
import jax.numpy as jnp
from jax import lax
from jax.experimental import pallas as pl
from jax.experimental.pallas import tpu as pltpu
from jax.sharding import PartitionSpec as P

HALF_ROWS = 4
HALF_COLS = 16
epsilon = 1e-06


def split(x):
    high = x.astype(jnp.bfloat16)
    low = (x - high.astype(jnp.float32)).astype(jnp.bfloat16)
    return high, low


def row_window(f, rows):
    length = f.shape[0]
    total, width = f, 1
    while width < 2 * HALF_ROWS:
        total = total + pltpu.roll(total, length - width, 0)
        width *= 2
    return total[:rows] + f[2 * HALF_ROWS:]


def kernel(counts, nd, own, stage, n_rows, *refs):
    def take(n):
        nonlocal refs
        head, refs = refs[:n], refs[n:]
        return head

    (plan_ref,) = take(0 if stage == "early" else 1)[:1] or (None,)
    own_ref, own_power, done = take(3) if stage == "last" else (None,) * 3
    edges, inners, rim_x, rim_c = (take(len(counts[n])) for n in (0, 0, 2, 1))
    (band_ref,) = take(1)
    if stage == "early":
        own_ref, own_power, buf, ext, res = refs
    elif stage == "last":
        out_ref, ext, res, buf, sems = refs
    else:
        out_ref, ext, res, buf, own_ref, own_power, sems = refs
    half = HALF_ROWS
    rows = inners[0].shape[2] + 2 * half
    first = nd if stage == "all" else 0
    slots = sum(counts[0]) - first
    row = lax.axis_index("row")
    odd = row % 2 == 1
    copies = []

    if stage == "last":
        listed = plan_ref[...]
        slot_of = ((listed // nd) ^ lax.axis_index("date")) * nd + listed % nd
        digits = (listed.shape[1] - 1).bit_length()
        each = 31 // digits
        lane = lax.broadcasted_iota(jnp.int32, listed.shape, 1)
        words = [
            jnp.sum(jnp.where(slot_of // each == w, lane << (slot_of % each * digits), 0))
            for w in range(-(-listed.shape[1] // each))
        ]

    def place(slot, date):
        if stage == "last":
            return (words[slot // each] >> (slot % each * digits)) & ((1 << digits) - 1)
        listed = plan_ref[...]
        lane = lax.broadcasted_iota(jnp.int32, listed.shape, 1)
        return jnp.sum(jnp.where(listed == date, lane, 0))

    def send(ref, slot):
        if stage == "all":
            date = pl.program_id(0) * slots + slot
        else:
            date = (lax.axis_index("date") ^ (slot // nd)) * nd + slot % nd
        k = place(slot, date)
        for d in range(nd):
            copy = pltpu.make_async_copy(ref[d], out_ref.at[d, k], sems.at[d, slot])
            copy.start()
            copies.append(copy)

    at = 0
    for ref, inner, count in zip(edges, inners, counts[0]):
        for d in range(count):
            to = own_ref.at[at] if stage != "last" and at < nd else ext.at[at]
            to[:, half:2 * half] = ref[d, :, half:]
            to[:, 2 * half:rows] = inner[d]
            to[:, rows:rows + half] = ref[d, :, :half]
            at += 1
    near = [r.at[d] for r, count in zip(rim_c, counts[1]) for d in range(count)]
    far = [r.at[d] for r, count in zip(rim_x, counts[2]) for d in range(count)]
    for at, (c, x) in enumerate(zip(near, far)):
        to = own_ref.at[at] if stage != "last" and at < nd else ext.at[at]
        top = jnp.where(odd, c[...], x[...])
        bottom = jnp.where(odd, x[...], c[...])
        to[:, :half] = jnp.where(row == 0, 0.0, top)
        to[:, rows + half:] = jnp.where(row == n_rows - 1, 0.0, bottom)

    band = band_ref[...]

    def columns(fields):
        high, low = zip(*(split(f) for f in fields))
        both = jnp.concatenate(high + low, axis=0)
        out = jnp.dot(both, band, preferred_element_type=jnp.float32)
        middle = out.shape[0] // 2
        return out[:middle] + out[middle:]

    def power_of(re, im):
        return row_window(re * re + im * im, rows)

    def cross_of(mr, mi, re, im):
        return [row_window(mr * re + mi * im, rows), row_window(mi * re - mr * im, rows)]

    def scale(a, b):
        return lax.rsqrt(a * b + epsilon)

    if stage != "last":
        fields = [power_of(own_ref[d, 0], own_ref[d, 1]) for d in range(nd)]
        pairs = [(d, s) for s in range(nd) for d in range(s)] if stage == "early" else []
        for d, s in pairs:
            fields += cross_of(own_ref[d, 0], own_ref[d, 1], own_ref[s, 0], own_ref[s, 1])
        sums = columns(fields)
        for d in range(nd):
            own_power[d] = sums[d * rows:(d + 1) * rows]
        if stage == "early":
            for d in range(nd):
                power = own_power[d]
                buf[d, d, 0] = power * scale(power, power)
                buf[d, d, 1] = jnp.zeros_like(power)
            for n, (d, s) in enumerate(pairs):
                at = (nd + 2 * n) * rows
                factor = scale(own_power[d], own_power[s])
                real, imag = sums[at:at + rows] * factor, sums[at + rows:at + 2 * rows] * factor
                buf[d, s, 0], buf[d, s, 1] = real, imag
                buf[s, d, 0], buf[s, d, 1] = real, -imag

    for s in range(nd if stage == "early" else 0, slots):
        re, im = ext[first + s, 0], ext[first + s, 1]
        fields = [power_of(re, im)]
        for d in range(nd):
            fields += cross_of(own_ref[d, 0], own_ref[d, 1], re, im)
        res[s] = columns(fields)
        power = res[s, :rows]
        for d in range(nd):
            factor = scale(own_power[d], power)
            at = (1 + 2 * d) * rows
            buf[d, s, 0] = res[s, at:at + rows] * factor
            buf[d, s, 1] = res[s, at + rows:at + 2 * rows] * factor
        if stage == "last" and s == 0:
            for t in range(own):
                send([done.at[d, t] for d in range(nd)], t)
        if stage != "early":
            send([buf.at[d, s] for d in range(nd)], own + s)
    for copy in copies:
        copy.wait()


def pairs_of(size, flip):
    return [(i, i ^ flip) for i in range(size)]


def body(stack_data, plan):
    nd, _, rows, cols = stack_data.shape
    size, n_rows = lax.axis_size("date"), lax.axis_size("row")
    half = HALF_ROWS
    odd = lax.axis_index("row") % 2 == 1

    near = [(i, i ^ 1) for i in range(n_rows) if (i ^ 1) < n_rows]
    far = [(i, (i + 1) % n_rows) for i in range(1, n_rows, 2)] if n_rows % 2 == 0 else [
        (i, i + 1) for i in range(1, n_rows - 1, 2)]
    far = far + [(j, i) for i, j in far if i != j]

    def cut(block):
        first, last = block[:, :, :half], block[:, :, rows - half:]
        return jnp.concatenate([last, first], axis=2), block[:, :, half:rows - half]

    def rim_near(edge):
        last, first = edge[:, :, :half], edge[:, :, half:]
        return lax.ppermute(jnp.where(odd, first, last), "row", near)

    def rim_far(edge):
        last, first = edge[:, :, :half], edge[:, :, half:]
        return lax.ppermute(jnp.where(odd, last, first), "row", far)

    def z(array, flip):
        return lax.ppermute(array, "date", pairs_of(size, flip))

    def after(array, *others):
        return lax.optimization_barrier((array,) + others)[0]

    def join(*blocks):
        return jnp.concatenate(blocks, axis=0)

    out_col = lax.broadcasted_iota(jnp.int32, (cols, cols), 0)
    in_col = lax.broadcasted_iota(jnp.int32, (cols, cols), 1)
    band = (jnp.abs(out_col - in_col) <= HALF_COLS).astype(jnp.bfloat16)
    out_shape = jax.ShapeDtypeStruct((nd, size * nd, 2, rows, cols), jnp.float32)
    own_shape = (nd, 2, rows + 2 * half, cols)
    power_shape = (nd, rows, cols)
    vmem = pl.BlockSpec(memory_space=pltpu.VMEM)
    listed = jnp.maximum(plan, 0).reshape(1, -1)
    hbm = pl.BlockSpec(memory_space=pl.ANY)

    def scratch(total, slots):
        return [
            pltpu.VMEM((total, 2, rows + 2 * half, cols), jnp.float32),
            pltpu.VMEM((slots, (1 + 2 * nd) * rows, cols), jnp.float32),
            pltpu.VMEM((nd, slots, 2, rows, cols), jnp.float32),
        ]

    def work(slots):
        pairs = slots * nd * rows * cols
        return pl.CostEstimate(flops=16 * pairs * cols, bytes_accessed=16 * pairs, transcendentals=pairs)

    params = pltpu.CompilerParams(vmem_limit_bytes=32 * 2**20)
    edge, inner = cut(stack_data)
    if size == 4:
        edge_2 = z(edge, 2)
        edge_1 = z(edge, 1)
        inner_2 = z(inner, 2)
        inner_1 = z(inner, 1)
        edge_3 = z(edge_2, 1)
        inner_3 = z(inner_2, 1)
        early = join(edge, edge_1, edge_2)
        near_a, far_a = rim_near(early), rim_far(early)
        near_b, far_b = rim_near(edge_3), rim_far(edge_3)
        slots = 3 * nd
        operands = [edge, edge_1, edge_2, inner, inner_1, inner_2, far_a, near_a, band]
        own, power, done = pl.pallas_call(
            functools.partial(kernel, ([nd] * 3, [slots], [slots]), nd, 0, "early", n_rows),
            out_shape=[
                jax.ShapeDtypeStruct(own_shape, jnp.float32),
                jax.ShapeDtypeStruct(power_shape, jnp.float32),
                jax.ShapeDtypeStruct((nd, slots, 2, rows, cols), jnp.float32),
            ],
            in_specs=[vmem] * len(operands),
            out_specs=[vmem] * 3,
            scratch_shapes=scratch(slots, slots)[:2],
            compiler_params=params,
            cost_estimate=work(slots),
            name="early_dates",
        )(*operands)
        operands = [listed, own, power, done, edge_3, inner_3, far_b, near_b, band]
        return pl.pallas_call(
            functools.partial(kernel, ([nd], [nd], [nd]), nd, slots, "last", n_rows),
            out_shape=out_shape,
            in_specs=[vmem] * len(operands),
            out_specs=hbm,
            scratch_shapes=scratch(nd, nd) + [pltpu.SemaphoreType.DMA((nd, size * nd))],
            compiler_params=params,
            cost_estimate=work(nd),
            name="last_dates",
        )(*operands)

    gathered = lax.all_gather(stack_data, "date", axis=0, tiled=True)
    all_edge, all_inner = cut(gathered)
    operands = [edge, all_edge, inner, all_inner, rim_far(edge), rim_far(all_edge), rim_near(edge), rim_near(all_edge)]
    slots = next(n for n in (8, 4, 2, 1) if (size * nd) % n == 0)

    def spec(array, chunk):
        if chunk:
            return pl.BlockSpec((slots,) + array.shape[1:], lambda g: (g, 0, 0, 0))
        return pl.BlockSpec(array.shape, lambda g: (0,) * array.ndim)

    return pl.pallas_call(
        functools.partial(kernel, ([nd, slots],) * 3, nd, 0, "all", n_rows),
        grid=(size * nd // slots,),
        out_shape=out_shape,
        in_specs=[vmem] + [spec(a, n % 2) for n, a in enumerate(operands)] + [spec(band, 0)],
        out_specs=hbm,
        scratch_shapes=scratch(nd + slots, slots)
        + [
            pltpu.VMEM(own_shape, jnp.float32),
            pltpu.VMEM(power_shape, jnp.float32),
            pltpu.SemaphoreType.DMA((nd, slots)),
        ],
        compiler_params=params,
        name="all_dates",
    )(listed, *operands, band)


def solution(mesh):
    placed = (P(("grp", "date"), None, "row", None), P())
    return jax.shard_map(
        body,
        mesh=mesh,
        in_specs=placed,
        out_specs=P(("grp", "date"), None, None, "row", None),
        check_vma=False,
    )
```

```python
import functools

import jax
import jax.numpy as jnp
from jax import lax
from jax.experimental import pallas as pl
from jax.experimental.pallas import tpu as pltpu
from jax.sharding import PartitionSpec as P

HALF_ROWS = 4
HALF_COLS = 16
epsilon = 1e-06


def split(x):
    high = x.astype(jnp.bfloat16)
    low = (x - high.astype(jnp.float32)).astype(jnp.bfloat16)
    return high, low


def row_window(f, rows):
    length = f.shape[0]
    total, width = f, 1
    while width < 2 * HALF_ROWS:
        total = total + pltpu.roll(total, length - width, 0)
        width *= 2
    return total[:rows] + f[2 * HALF_ROWS:]


def kernel(counts, nd, own, stage, n_rows, digits, *refs):
    def take(n):
        nonlocal refs
        head, refs = refs[:n], refs[n:]
        return head

    each = 31 // digits
    (plan_ref,) = take(1)
    own_ref, own_power, done = take(3) if stage == "last" else (None,) * 3
    edges, inners, rim_c, rim_x = (take(len(counts[n])) for n in (0, 0, 1, 2))
    (band_ref,) = take(1)
    if stage == "early":
        own_ref, own_power, buf, words_ref, ext, res = refs
    elif stage == "last":
        out_ref, ext, res, buf, sems = refs
    else:
        out_ref, ext, res, buf, own_ref, own_power, sems = refs
    half = HALF_ROWS
    rows = inners[0].shape[2] + 2 * half
    first = nd if stage == "all" else 0
    slots = sum(counts[0]) - first
    row = lax.axis_index("row")
    odd = row % 2 == 1
    copies = []

    if stage == "early":
        listed = plan_ref[...]
        slot_of = ((listed // nd) ^ lax.axis_index("date")) * nd + listed % nd
        lane = lax.broadcasted_iota(jnp.int32, listed.shape, 1)
        for w in range(words_ref.shape[0]):
            word = jnp.where(slot_of // each == w, lane << (slot_of % each * digits), 0)
            words_ref[w:w + 1] = jnp.broadcast_to(jnp.sum(word, axis=1, keepdims=True), (1, words_ref.shape[1]))
    elif stage == "last":
        words = [jnp.max(plan_ref[w:w + 1, :1]) for w in range(plan_ref.shape[0])]

    def place(slot, date):
        if stage == "last":
            return (words[slot // each] >> (slot % each * digits)) & ((1 << digits) - 1)
        listed = plan_ref[...]
        lane = lax.broadcasted_iota(jnp.int32, listed.shape, 1)
        return jnp.sum(jnp.where(listed == date, lane, 0))

    def send(ref, slot):
        if stage == "all":
            date = pl.program_id(0) * slots + slot
        else:
            date = (lax.axis_index("date") ^ (slot // nd)) * nd + slot % nd
        k = place(slot, date)
        for d in range(nd):
            copy = pltpu.make_async_copy(ref[d], out_ref.at[d, k], sems.at[d, slot])
            copy.start()
            copies.append(copy)

    at = 0
    for ref, inner, count in zip(edges, inners, counts[0]):
        for d in range(count):
            to = own_ref.at[at] if stage != "last" and at < nd else ext.at[at]
            to[:, half:2 * half] = ref[d, :, half:]
            to[:, 2 * half:rows] = inner[d]
            to[:, rows:rows + half] = ref[d, :, :half]
            at += 1
    near = [r.at[d] for r, count in zip(rim_c, counts[1]) for d in range(count)]
    far = [r.at[d] for r, count in zip(rim_x, counts[2]) for d in range(count)]
    for at, (c, x) in enumerate(zip(near, far)):
        to = own_ref.at[at] if stage != "last" and at < nd else ext.at[at]
        top = jnp.where(odd, c[...], x[...])
        bottom = jnp.where(odd, x[...], c[...])
        to[:, :half] = jnp.where(row == 0, 0.0, top)
        to[:, rows + half:] = jnp.where(row == n_rows - 1, 0.0, bottom)

    band = band_ref[...]

    def columns(fields):
        high, low = zip(*(split(f) for f in fields))
        both = jnp.concatenate(high + low, axis=0)
        out = jnp.dot(both, band, preferred_element_type=jnp.float32)
        middle = out.shape[0] // 2
        return out[:middle] + out[middle:]

    def power_of(re, im):
        return row_window(re * re + im * im, rows)

    def cross_of(mr, mi, re, im):
        return [row_window(mr * re + mi * im, rows), row_window(mi * re - mr * im, rows)]

    def scale(a, b):
        return lax.rsqrt(a * b + epsilon)

    if stage != "last":
        fields = [power_of(own_ref[d, 0], own_ref[d, 1]) for d in range(nd)]
        pairs = [(d, s) for s in range(nd) for d in range(s)] if stage == "early" else []
        for d, s in pairs:
            fields += cross_of(own_ref[d, 0], own_ref[d, 1], own_ref[s, 0], own_ref[s, 1])
        sums = columns(fields)
        for d in range(nd):
            own_power[d] = sums[d * rows:(d + 1) * rows]
        if stage == "early":
            for d in range(nd):
                power = own_power[d]
                buf[d, d, 0] = power * scale(power, power)
                buf[d, d, 1] = jnp.zeros_like(power)
            for n, (d, s) in enumerate(pairs):
                at = (nd + 2 * n) * rows
                factor = scale(own_power[d], own_power[s])
                real, imag = sums[at:at + rows] * factor, sums[at + rows:at + 2 * rows] * factor
                buf[d, s, 0], buf[d, s, 1] = real, imag
                buf[s, d, 0], buf[s, d, 1] = real, -imag

    for s in range(nd if stage == "early" else 0, slots):
        re, im = ext[first + s, 0], ext[first + s, 1]
        fields = [power_of(re, im)]
        for d in range(nd):
            fields += cross_of(own_ref[d, 0], own_ref[d, 1], re, im)
        res[s] = columns(fields)
        power = res[s, :rows]
        for d in range(nd):
            factor = scale(own_power[d], power)
            at = (1 + 2 * d) * rows
            buf[d, s, 0] = res[s, at:at + rows] * factor
            buf[d, s, 1] = res[s, at + rows:at + 2 * rows] * factor
        if stage == "last" and s == 0:
            for t in range(own):
                send([done.at[d, t] for d in range(nd)], t)
        if stage != "early":
            send([buf.at[d, s] for d in range(nd)], own + s)
    for copy in copies:
        copy.wait()


def pairs_of(size, flip):
    return [(i, i ^ flip) for i in range(size)]


def body(stack_data, plan):
    nd, _, rows, cols = stack_data.shape
    size, n_rows = lax.axis_size("date"), lax.axis_size("row")
    half = HALF_ROWS
    odd = lax.axis_index("row") % 2 == 1

    near = [(i, i ^ 1) for i in range(n_rows) if (i ^ 1) < n_rows]
    far = [(i, (i + 1) % n_rows) for i in range(1, n_rows, 2)] if n_rows % 2 == 0 else [
        (i, i + 1) for i in range(1, n_rows - 1, 2)]
    far = far + [(j, i) for i, j in far if i != j]

    def cut(block):
        first, last = block[:, :, :half], block[:, :, rows - half:]
        return jnp.concatenate([last, first], axis=2), block[:, :, half:rows - half]

    def rim_near(edge):
        last, first = edge[:, :, :half], edge[:, :, half:]
        return lax.ppermute(jnp.where(odd, first, last), "row", near)

    def rim_far(edge):
        last, first = edge[:, :, :half], edge[:, :, half:]
        return lax.ppermute(jnp.where(odd, last, first), "row", far)

    def across(edge, flip):
        last, first = edge[:, :, :half], edge[:, :, half:]
        pairs = [((d ^ flip) * n_rows + j, d * n_rows + i) for d in range(size) for i, j in far]
        return lax.ppermute(jnp.where(odd, last, first), ("date", "row"), pairs)

    def z(array, flip):
        return lax.ppermute(array, "date", pairs_of(size, flip))

    def after(array, *others):
        return lax.optimization_barrier((array,) + others)[0]

    def after(array, *others):
        return lax.optimization_barrier((array,) + others)[0]

    def join(*blocks):
        return jnp.concatenate(blocks, axis=0)

    out_col = lax.broadcasted_iota(jnp.int32, (cols, cols), 0)
    in_col = lax.broadcasted_iota(jnp.int32, (cols, cols), 1)
    band = (jnp.abs(out_col - in_col) <= HALF_COLS).astype(jnp.bfloat16)
    out_shape = jax.ShapeDtypeStruct((nd, size * nd, 2, rows, cols), jnp.float32)
    own_shape = (nd, 2, rows + 2 * half, cols)
    power_shape = (nd, rows, cols)
    vmem = pl.BlockSpec(memory_space=pltpu.VMEM)
    listed = jnp.maximum(plan, 0).reshape(1, -1)
    digits = max(1, (size * nd - 1).bit_length())
    hbm = pl.BlockSpec(memory_space=pl.ANY)

    def scratch(total, slots):
        return [
            pltpu.VMEM((total, 2, rows + 2 * half, cols), jnp.float32),
            pltpu.VMEM((slots, (1 + 2 * nd) * rows, cols), jnp.float32),
            pltpu.VMEM((nd, slots, 2, rows, cols), jnp.float32),
        ]

    def work(slots):
        pairs = slots * nd * rows * cols
        return pl.CostEstimate(flops=16 * pairs * cols, bytes_accessed=16 * pairs, transcendentals=pairs)

    params = pltpu.CompilerParams(vmem_limit_bytes=32 * 2**20)
    edge, inner = cut(stack_data)
    if size == 4:
        edge_2 = z(edge, 2)
        inner_2 = z(inner, 2)
        edge_1 = z(edge, 1)
        inner_1 = z(inner, 1)
        edge_3 = z(edge_2, 1)
        inner_3 = z(inner_2, 1)
        early = join(edge, edge_1, edge_2)
        far_a = rim_far(early)
        far_b = across(edge_2, 1)
        near_a, near_b = rim_near(early), rim_near(after(edge_3, inner_1))
        slots = 3 * nd
        operands = [listed, edge, edge_1, edge_2, inner, inner_1, inner_2, near_a, far_a, band]
        own, power, done, words = pl.pallas_call(
            functools.partial(kernel, ([nd] * 3, [slots], [slots]), nd, 0, "early", n_rows, digits),
            out_shape=[
                jax.ShapeDtypeStruct(own_shape, jnp.float32),
                jax.ShapeDtypeStruct(power_shape, jnp.float32),
                jax.ShapeDtypeStruct((nd, slots, 2, rows, cols), jnp.float32),
                jax.ShapeDtypeStruct((-(-size * nd // (31 // digits)), 128), jnp.int32),
            ],
            in_specs=[vmem] * len(operands),
            out_specs=[vmem] * 4,
            scratch_shapes=scratch(slots, slots)[:2],
            compiler_params=params,
            cost_estimate=work(slots),
            name="early_dates",
        )(*operands)
        operands = [words, own, power, done, edge_3, inner_3, near_b, far_b, band]
        return pl.pallas_call(
            functools.partial(kernel, ([nd], [nd], [nd]), nd, slots, "last", n_rows, digits),
            out_shape=out_shape,
            in_specs=[vmem] * len(operands),
            out_specs=hbm,
            scratch_shapes=scratch(nd, nd) + [pltpu.SemaphoreType.DMA((nd, size * nd))],
            compiler_params=params,
            cost_estimate=work(nd),
            name="last_dates",
        )(*operands)

    gathered = lax.all_gather(stack_data, "date", axis=0, tiled=True)
    all_edge, all_inner = cut(gathered)
    operands = [edge, all_edge, inner, all_inner, rim_near(edge), rim_near(all_edge), rim_far(edge), rim_far(all_edge)]
    slots = next(n for n in (8, 4, 2, 1) if (size * nd) % n == 0)

    def spec(array, chunk):
        if chunk:
            return pl.BlockSpec((slots,) + array.shape[1:], lambda g: (g, 0, 0, 0))
        return pl.BlockSpec(array.shape, lambda g: (0,) * array.ndim)

    return pl.pallas_call(
        functools.partial(kernel, ([nd, slots],) * 3, nd, 0, "all", n_rows, digits),
        grid=(size * nd // slots,),
        out_shape=out_shape,
        in_specs=[vmem] + [spec(a, n % 2) for n, a in enumerate(operands)] + [spec(band, 0)],
        out_specs=hbm,
        scratch_shapes=scratch(nd + slots, slots)
        + [
            pltpu.VMEM(own_shape, jnp.float32),
            pltpu.VMEM(power_shape, jnp.float32),
            pltpu.SemaphoreType.DMA((nd, slots)),
        ],
        compiler_params=params,
        name="all_dates",
    )(listed, *operands, band)


def solution(mesh):
    placed = (P(("grp", "date"), None, "row", None), P())
    return jax.shard_map(
        body,
        mesh=mesh,
        in_specs=placed,
        out_specs=P(("grp", "date"), None, None, "row", None),
        check_vma=False,
    )
```

```python
import functools

import jax
import jax.numpy as jnp
from jax import lax
from jax.experimental import pallas as pl
from jax.experimental.pallas import tpu as pltpu
from jax.sharding import PartitionSpec as P

HALF_ROWS = 4
HALF_COLS = 16
LANES = 128
epsilon = 1e-06


def split(x):
    high = x.astype(jnp.bfloat16)
    low = (x - high.astype(jnp.float32)).astype(jnp.bfloat16)
    return high, low


def row_window(f, rows):
    length = f.shape[0]
    total, width = f, 1
    while width < 2 * HALF_ROWS:
        total = total + pltpu.roll(total, length - width, 0)
        width *= 2
    return total[:rows] + f[2 * HALF_ROWS:]


def kernel(counts, nd, own, stage, n_rows, digits, *refs):
    def take(n):
        nonlocal refs
        head, refs = refs[:n], refs[n:]
        return head

    each = 31 // digits
    (plan_ref,) = take(1)
    own_ref, own_power, done = take(3) if stage == "last" else (None,) * 3
    edges, inners, rim_c, rim_x = (take(len(counts[n])) for n in (0, 0, 1, 2))
    (band_ref,) = take(1)
    if stage == "early":
        own_ref, own_power, buf, words_ref, ext, res = refs
    elif stage == "last":
        out_ref, ext, res, buf, sems = refs
    else:
        out_ref, ext, res, buf, own_ref, own_power, sems = refs
    half = HALF_ROWS
    rows = inners[0].shape[2] + 2 * half
    first = nd if stage == "all" else 0
    slots = sum(counts[0]) - first
    row = lax.axis_index("row")
    odd = row % 2 == 1
    copies = []

    if stage == "early":
        listed = plan_ref[...]
        slot_of = ((listed // nd) ^ lax.axis_index("date")) * nd + listed % nd
        lane = lax.broadcasted_iota(jnp.int32, listed.shape, 1)
        for w in range(words_ref.shape[0]):
            word = jnp.where(slot_of // each == w, lane << (slot_of % each * digits), 0)
            words_ref[w:w + 1] = jnp.broadcast_to(jnp.sum(word, axis=1, keepdims=True), (1, words_ref.shape[1]))
    elif stage == "last":
        words = [jnp.max(plan_ref[w:w + 1, :1]) for w in range(plan_ref.shape[0])]

    def place(slot, date):
        if stage == "last":
            return (words[slot // each] >> (slot % each * digits)) & ((1 << digits) - 1)
        listed = plan_ref[...]
        lane = lax.broadcasted_iota(jnp.int32, listed.shape, 1)
        return jnp.sum(jnp.where(listed == date, lane, 0))

    def send(ref, slot):
        if stage == "all":
            date = pl.program_id(0) * slots + slot
        else:
            date = (lax.axis_index("date") ^ (slot // nd)) * nd + slot % nd
        k = place(slot, date)
        copy = pltpu.make_async_copy(ref, out_ref.at[:, k], sems.at[slot])
        copy.start()
        copies.append(copy)

    at = 0
    for ref, inner, count in zip(edges, inners, counts[0]):
        for d in range(count):
            to = own_ref.at[at] if stage != "last" and at < nd else ext.at[at]
            to[:, half:2 * half] = ref[d, :, half:]
            to[:, 2 * half:rows] = inner[d]
            to[:, rows:rows + half] = ref[d, :, :half]
            at += 1
    near = [r.at[d] for r, count in zip(rim_c, counts[1]) for d in range(count)]
    far = [r.at[d] for r, count in zip(rim_x, counts[2]) for d in range(count)]
    for at, (c, x) in enumerate(zip(near, far)):
        to = own_ref.at[at] if stage != "last" and at < nd else ext.at[at]
        top = jnp.where(odd, c[...], x[...])
        bottom = jnp.where(odd, x[...], c[...])
        to[:, :half] = jnp.where(row == 0, 0.0, top)
        to[:, rows + half:] = jnp.where(row == n_rows - 1, 0.0, bottom)

    band = band_ref[...]

    def columns(fields):
        high, low = zip(*(split(f) for f in fields))
        both = jnp.concatenate(high + low, axis=0)
        tiles = both.shape[1] // LANES
        height = both.shape[0] // 2
        lane = lax.broadcasted_iota(jnp.int32, (height, LANES), 1)
        parts = []
        for t in range(tiles - 1):
            out = jnp.dot(both[:, t * LANES:(t + 2) * LANES], band, preferred_element_type=jnp.float32)
            parts.append(out[:height] + out[height:])
        sums = [parts[0][:, :LANES]]
        for t in range(1, tiles - 1):
            sums.append(jnp.where(lane < LANES // 2, parts[t - 1][:, LANES:], parts[t][:, :LANES]))
        sums.append(parts[-1][:, LANES:])
        return jnp.concatenate(sums, axis=1)

    def power_of(re, im):
        return row_window(re * re + im * im, rows)

    def cross_of(mr, mi, re, im):
        return [row_window(mr * re + mi * im, rows), row_window(mi * re - mr * im, rows)]

    def scale(a, b):
        return lax.rsqrt(a * b + epsilon)

    if stage != "last":
        fields = [power_of(own_ref[d, 0], own_ref[d, 1]) for d in range(nd)]
        pairs = [(d, s) for s in range(nd) for d in range(s)] if stage == "early" else []
        for d, s in pairs:
            fields += cross_of(own_ref[d, 0], own_ref[d, 1], own_ref[s, 0], own_ref[s, 1])
        sums = columns(fields)
        for d in range(nd):
            own_power[d] = sums[d * rows:(d + 1) * rows]
        if stage == "early":
            for d in range(nd):
                power = own_power[d]
                buf[d, d, 0] = power * scale(power, power)
                buf[d, d, 1] = jnp.zeros_like(power)
            for n, (d, s) in enumerate(pairs):
                at = (nd + 2 * n) * rows
                factor = scale(own_power[d], own_power[s])
                real, imag = sums[at:at + rows] * factor, sums[at + rows:at + 2 * rows] * factor
                buf[d, s, 0], buf[d, s, 1] = real, imag
                buf[s, d, 0], buf[s, d, 1] = real, -imag

    for s in range(nd if stage == "early" else 0, slots):
        re, im = ext[first + s, 0], ext[first + s, 1]
        fields = [power_of(re, im)]
        for d in range(nd):
            fields += cross_of(own_ref[d, 0], own_ref[d, 1], re, im)
        res[s] = columns(fields)
        power = res[s, :rows]
        for d in range(nd):
            factor = scale(own_power[d], power)
            at = (1 + 2 * d) * rows
            buf[d, s, 0] = res[s, at:at + rows] * factor
            buf[d, s, 1] = res[s, at + rows:at + 2 * rows] * factor
        if stage == "last" and s == 0:
            for t in range(own):
                send(done.at[:, t], t)
        if stage != "early":
            send(buf.at[:, s], own + s)
    for copy in copies:
        copy.wait()


def pairs_of(size, flip):
    return [(i, i ^ flip) for i in range(size)]


def body(stack_data, plan):
    nd, _, rows, cols = stack_data.shape
    size, n_rows = lax.axis_size("date"), lax.axis_size("row")
    half = HALF_ROWS
    odd = lax.axis_index("row") % 2 == 1

    near = [(i, i ^ 1) for i in range(n_rows) if (i ^ 1) < n_rows]
    far = [(i, (i + 1) % n_rows) for i in range(1, n_rows, 2)] if n_rows % 2 == 0 else [
        (i, i + 1) for i in range(1, n_rows - 1, 2)]
    far = far + [(j, i) for i, j in far if i != j]

    def cut(block):
        first, last = block[:, :, :half], block[:, :, rows - half:]
        return jnp.concatenate([last, first], axis=2), block[:, :, half:rows - half]

    def rim_near(edge):
        last, first = edge[:, :, :half], edge[:, :, half:]
        return lax.ppermute(jnp.where(odd, first, last), "row", near)

    def rim_far(edge):
        last, first = edge[:, :, :half], edge[:, :, half:]
        return lax.ppermute(jnp.where(odd, last, first), "row", far)

    def across(edge, flip):
        last, first = edge[:, :, :half], edge[:, :, half:]
        pairs = [((d ^ flip) * n_rows + j, d * n_rows + i) for d in range(size) for i, j in far]
        return lax.ppermute(jnp.where(odd, last, first), ("date", "row"), pairs)

    def z(array, flip):
        return lax.ppermute(array, "date", pairs_of(size, flip))

    def after(array, *others):
        return lax.optimization_barrier((array,) + others)[0]

    def after(array, *others):
        return lax.optimization_barrier((array,) + others)[0]

    def join(*blocks):
        return jnp.concatenate(blocks, axis=0)

    out_col = lax.broadcasted_iota(jnp.int32, (2 * LANES, 2 * LANES), 0)
    in_col = lax.broadcasted_iota(jnp.int32, (2 * LANES, 2 * LANES), 1)
    band = (jnp.abs(out_col - in_col) <= HALF_COLS).astype(jnp.bfloat16)
    out_shape = jax.ShapeDtypeStruct((nd, size * nd, 2, rows, cols), jnp.float32)
    own_shape = (nd, 2, rows + 2 * half, cols)
    power_shape = (nd, rows, cols)
    vmem = pl.BlockSpec(memory_space=pltpu.VMEM)
    listed = jnp.maximum(plan, 0).reshape(1, -1)
    digits = max(1, (size * nd - 1).bit_length())
    hbm = pl.BlockSpec(memory_space=pl.ANY)

    def scratch(total, slots):
        return [
            pltpu.VMEM((total, 2, rows + 2 * half, cols), jnp.float32),
            pltpu.VMEM((slots, (1 + 2 * nd) * rows, cols), jnp.float32),
            pltpu.VMEM((nd, slots, 2, rows, cols), jnp.float32),
        ]

    def work(slots):
        pairs = slots * nd * rows * cols
        return pl.CostEstimate(flops=16 * pairs * cols, bytes_accessed=16 * pairs, transcendentals=pairs)

    params = pltpu.CompilerParams(vmem_limit_bytes=32 * 2**20)
    edge, inner = cut(stack_data)
    if size == 4:
        edge_2 = z(edge, 2)
        inner_2 = z(inner, 2)
        edge_1 = z(edge, 1)
        inner_1 = z(inner, 1)
        edge_3 = z(edge_2, 1)
        inner_3 = z(inner_2, 1)
        early = join(edge, edge_1, edge_2)
        far_a = rim_far(early)
        far_b = across(edge_2, 1)
        near_a, near_b = rim_near(early), rim_near(after(edge_3, inner_1))
        slots = 3 * nd
        operands = [listed, edge, edge_1, edge_2, inner, inner_1, inner_2, near_a, far_a, band]
        own, power, done, words = pl.pallas_call(
            functools.partial(kernel, ([nd] * 3, [slots], [slots]), nd, 0, "early", n_rows, digits),
            out_shape=[
                jax.ShapeDtypeStruct(own_shape, jnp.float32),
                jax.ShapeDtypeStruct(power_shape, jnp.float32),
                jax.ShapeDtypeStruct((nd, slots, 2, rows, cols), jnp.float32),
                jax.ShapeDtypeStruct((-(-size * nd // (31 // digits)), 128), jnp.int32),
            ],
            in_specs=[vmem] * len(operands),
            out_specs=[vmem] * 4,
            scratch_shapes=scratch(slots, slots)[:2],
            compiler_params=params,
            cost_estimate=work(slots),
            name="early_dates",
        )(*operands)
        operands = [words, own, power, done, edge_3, inner_3, near_b, far_b, band]
        return pl.pallas_call(
            functools.partial(kernel, ([nd], [nd], [nd]), nd, slots, "last", n_rows, digits),
            out_shape=out_shape,
            in_specs=[vmem] * len(operands),
            out_specs=hbm,
            scratch_shapes=scratch(nd, nd) + [pltpu.SemaphoreType.DMA((size * nd,))],
            compiler_params=params,
            cost_estimate=work(nd),
            name="last_dates",
        )(*operands)

    gathered = lax.all_gather(stack_data, "date", axis=0, tiled=True)
    all_edge, all_inner = cut(gathered)
    operands = [edge, all_edge, inner, all_inner, rim_near(edge), rim_near(all_edge), rim_far(edge), rim_far(all_edge)]
    slots = next(n for n in (8, 4, 2, 1) if (size * nd) % n == 0)

    def spec(array, chunk):
        if chunk:
            return pl.BlockSpec((slots,) + array.shape[1:], lambda g: (g, 0, 0, 0))
        return pl.BlockSpec(array.shape, lambda g: (0,) * array.ndim)

    return pl.pallas_call(
        functools.partial(kernel, ([nd, slots],) * 3, nd, 0, "all", n_rows, digits),
        grid=(size * nd // slots,),
        out_shape=out_shape,
        in_specs=[vmem] + [spec(a, n % 2) for n, a in enumerate(operands)] + [spec(band, 0)],
        out_specs=hbm,
        scratch_shapes=scratch(nd + slots, slots)
        + [
            pltpu.VMEM(own_shape, jnp.float32),
            pltpu.VMEM(power_shape, jnp.float32),
            pltpu.SemaphoreType.DMA((slots,)),
        ],
        compiler_params=params,
        name="all_dates",
    )(listed, *operands, band)


def solution(mesh):
    placed = (P(("grp", "date"), None, "row", None), P())
    return jax.shard_map(
        body,
        mesh=mesh,
        in_specs=placed,
        out_specs=P(("grp", "date"), None, None, "row", None),
        check_vma=False,
    )
```

```python
import functools

import jax
import jax.numpy as jnp
from jax import lax
from jax.experimental import pallas as pl
from jax.experimental.pallas import tpu as pltpu
from jax.sharding import PartitionSpec as P

HALF_ROWS = 4
HALF_COLS = 16
LANES = 128
epsilon = 1e-06


def split(x):
    high = x.astype(jnp.bfloat16)
    low = (x - high.astype(jnp.float32)).astype(jnp.bfloat16)
    return high, low


def row_window(f, rows):
    length = f.shape[0]
    total, width = f, 1
    while width < 2 * HALF_ROWS:
        total = total + pltpu.roll(total, length - width, 0)
        width *= 2
    return total[:rows] + f[2 * HALF_ROWS:]


def kernel(counts, nd, own, stage, n_rows, digits, *refs):
    def take(n):
        nonlocal refs
        head, refs = refs[:n], refs[n:]
        return head

    each = 31 // digits
    (plan_ref,) = take(1)
    own_ref, own_power, done = take(3) if stage == "last" else (None,) * 3
    edges, inners, rim_c, rim_x = (take(len(counts[n])) for n in (0, 0, 1, 2))
    (band_ref,) = take(1)
    if stage == "early":
        own_ref, own_power, buf, words_ref, ext, res = refs
    elif stage == "last":
        out_ref, ext, res, buf, sems = refs
    else:
        out_ref, ext, res, buf, own_ref, own_power, sems = refs
    half = HALF_ROWS
    rows = inners[0].shape[2] + 2 * half
    first = nd if stage == "all" else 0
    slots = sum(counts[0]) - first
    row = lax.axis_index("row")
    odd = row % 2 == 1
    copies = []

    if stage == "early":
        listed = plan_ref[...]
        slot_of = ((listed // nd) ^ lax.axis_index("date")) * nd + listed % nd
        lane = lax.broadcasted_iota(jnp.int32, listed.shape, 1)
        for w in range(words_ref.shape[0]):
            word = jnp.where(slot_of // each == w, lane << (slot_of % each * digits), 0)
            words_ref[w:w + 1] = jnp.broadcast_to(jnp.sum(word, axis=1, keepdims=True), (1, words_ref.shape[1]))
    elif stage == "last":
        words = [jnp.max(plan_ref[w:w + 1, :1]) for w in range(plan_ref.shape[0])]

    def place(slot, date):
        if stage == "last":
            return (words[slot // each] >> (slot % each * digits)) & ((1 << digits) - 1)
        listed = plan_ref[...]
        lane = lax.broadcasted_iota(jnp.int32, listed.shape, 1)
        return jnp.sum(jnp.where(listed == date, lane, 0))

    def send(ref, slot):
        if stage == "all":
            date = pl.program_id(0) * slots + slot
        else:
            date = (lax.axis_index("date") ^ (slot // nd)) * nd + slot % nd
        k = place(slot, date)
        copy = pltpu.make_async_copy(ref, out_ref.at[:, k], sems.at[slot])
        copy.start()
        copies.append(copy)

    at = 0
    for ref, inner, count in zip(edges, inners, counts[0]):
        for d in range(count):
            to = own_ref.at[at] if stage != "last" and at < nd else ext.at[at]
            to[:, half:2 * half] = ref[d, :, half:]
            to[:, 2 * half:rows] = inner[d]
            to[:, rows:rows + half] = ref[d, :, :half]
            at += 1
    near = [r.at[d] for r, count in zip(rim_c, counts[1]) for d in range(count)]
    far = [r.at[d] for r, count in zip(rim_x, counts[2]) for d in range(count)]
    for at, (c, x) in enumerate(zip(near, far)):
        to = own_ref.at[at] if stage != "last" and at < nd else ext.at[at]
        top = jnp.where(odd, c[...], x[...])
        bottom = jnp.where(odd, x[...], c[...])
        to[:, :half] = jnp.where(row == 0, 0.0, top)
        to[:, rows + half:] = jnp.where(row == n_rows - 1, 0.0, bottom)

    band = band_ref[...]

    def columns(fields):
        high, low = zip(*(split(f) for f in fields))
        both = jnp.concatenate(high + low, axis=0)
        tiles = both.shape[1] // LANES
        height = both.shape[0] // 2
        lane = lax.broadcasted_iota(jnp.int32, (height, LANES), 1)
        parts = []
        for t in range(tiles - 1):
            out = jnp.dot(both[:, t * LANES:(t + 2) * LANES], band, preferred_element_type=jnp.float32)
            parts.append(out[:height] + out[height:])
        sums = [parts[0][:, :LANES]]
        for t in range(1, tiles - 1):
            sums.append(jnp.where(lane < LANES // 2, parts[t - 1][:, LANES:], parts[t][:, :LANES]))
        sums.append(parts[-1][:, LANES:])
        return jnp.concatenate(sums, axis=1)

    def power_of(re, im):
        return row_window(re * re + im * im, rows)

    def cross_of(mr, mi, re, im):
        return [row_window(mr * re + mi * im, rows), row_window(mi * re - mr * im, rows)]

    def scale(a, b):
        return lax.rsqrt(a * b + epsilon)

    if stage != "last":
        fields = [power_of(own_ref[d, 0], own_ref[d, 1]) for d in range(nd)]
        pairs = [(d, s) for s in range(nd) for d in range(s)] if stage == "early" else []
        for d, s in pairs:
            fields += cross_of(own_ref[d, 0], own_ref[d, 1], own_ref[s, 0], own_ref[s, 1])
        sums = columns(fields)
        for d in range(nd):
            own_power[d] = sums[d * rows:(d + 1) * rows]
        if stage == "early":
            for d in range(nd):
                power = own_power[d]
                buf[d, d, 0] = power * scale(power, power)
                buf[d, d, 1] = jnp.zeros_like(power)
            for n, (d, s) in enumerate(pairs):
                at = (nd + 2 * n) * rows
                factor = scale(own_power[d], own_power[s])
                real, imag = sums[at:at + rows] * factor, sums[at + rows:at + 2 * rows] * factor
                buf[d, s, 0], buf[d, s, 1] = real, imag
                buf[s, d, 0], buf[s, d, 1] = real, -imag

    for s in range(nd if stage == "early" else 0, slots):
        re, im = ext[first + s, 0], ext[first + s, 1]
        fields = [power_of(re, im)]
        for d in range(nd):
            fields += cross_of(own_ref[d, 0], own_ref[d, 1], re, im)
        res[s] = columns(fields)
        power = res[s, :rows]
        for d in range(nd):
            factor = scale(own_power[d], power)
            at = (1 + 2 * d) * rows
            buf[d, s, 0] = res[s, at:at + rows] * factor
            buf[d, s, 1] = res[s, at + rows:at + 2 * rows] * factor
        if stage == "last" and s == 0:
            for t in range(own):
                send(done.at[:, t], t)
        if stage != "early":
            send(buf.at[:, s], own + s)
    for copy in copies:
        copy.wait()


def pairs_of(size, flip):
    return [(i, i ^ flip) for i in range(size)]


def body(stack_data, plan):
    nd, _, rows, cols = stack_data.shape
    size, n_rows = lax.axis_size("date"), lax.axis_size("row")
    half = HALF_ROWS
    odd = lax.axis_index("row") % 2 == 1

    near = [(i, i ^ 1) for i in range(n_rows) if (i ^ 1) < n_rows]
    far = [(i, (i + 1) % n_rows) for i in range(1, n_rows, 2)] if n_rows % 2 == 0 else [
        (i, i + 1) for i in range(1, n_rows - 1, 2)]
    far = far + [(j, i) for i, j in far if i != j]

    def cut(block):
        first, last = block[:, :, :half], block[:, :, rows - half:]
        return jnp.concatenate([last, first], axis=2), block[:, :, half:rows - half]

    def rim_near(edge):
        last, first = edge[:, :, :half], edge[:, :, half:]
        return lax.ppermute(jnp.where(odd, first, last), "row", near)

    def rim_far(edge):
        last, first = edge[:, :, :half], edge[:, :, half:]
        return lax.ppermute(jnp.where(odd, last, first), "row", far)

    def across(edge, flip):
        last, first = edge[:, :, :half], edge[:, :, half:]
        pairs = [((d ^ flip) * n_rows + j, d * n_rows + i) for d in range(size) for i, j in far]
        return lax.ppermute(jnp.where(odd, last, first), ("date", "row"), pairs)

    def z(array, flip):
        return lax.ppermute(array, "date", pairs_of(size, flip))

    def after(array, *others):
        return lax.optimization_barrier((array,) + others)[0]

    def after(array, *others):
        return lax.optimization_barrier((array,) + others)[0]

    def join(*blocks):
        return jnp.concatenate(blocks, axis=0)

    out_col = lax.broadcasted_iota(jnp.int32, (2 * LANES, 2 * LANES), 0)
    in_col = lax.broadcasted_iota(jnp.int32, (2 * LANES, 2 * LANES), 1)
    band = (jnp.abs(out_col - in_col) <= HALF_COLS).astype(jnp.bfloat16)
    out_shape = jax.ShapeDtypeStruct((nd, size * nd, 2, rows, cols), jnp.float32)
    own_shape = (nd, 2, rows + 2 * half, cols)
    power_shape = (nd, rows, cols)
    vmem = pl.BlockSpec(memory_space=pltpu.VMEM)
    listed = jnp.maximum(plan, 0).reshape(1, -1)
    digits = max(1, (size * nd - 1).bit_length())
    hbm = pl.BlockSpec(memory_space=pl.ANY)

    def scratch(total, slots):
        return [
            pltpu.VMEM((total, 2, rows + 2 * half, cols), jnp.float32),
            pltpu.VMEM((slots, (1 + 2 * nd) * rows, cols), jnp.float32),
            pltpu.VMEM((nd, slots, 2, rows, cols), jnp.float32),
        ]

    def work(slots):
        pairs = slots * nd * rows * cols
        return pl.CostEstimate(flops=16 * pairs * cols, bytes_accessed=16 * pairs, transcendentals=pairs)

    params = pltpu.CompilerParams(vmem_limit_bytes=32 * 2**20)
    edge, inner = cut(stack_data)
    if size == 4:
        edge_2 = z(edge, 2)
        inner_2 = z(inner, 2)
        edge_1 = z(edge, 1)
        inner_1 = z(after(inner, edge), 1)
        far_b = across(edge_2, 1)
        edge_3 = z(edge_2, 1)
        inner_3 = z(inner_2, 1)
        early = join(edge, edge_1, edge_2)
        far_a = rim_far(early)
        near_a, near_b = rim_near(early), rim_near(after(edge_3, inner_1))
        slots = 3 * nd
        operands = [listed, edge, edge_1, edge_2, inner, inner_1, inner_2, near_a, far_a, band]
        own, power, done, words = pl.pallas_call(
            functools.partial(kernel, ([nd] * 3, [slots], [slots]), nd, 0, "early", n_rows, digits),
            out_shape=[
                jax.ShapeDtypeStruct(own_shape, jnp.float32),
                jax.ShapeDtypeStruct(power_shape, jnp.float32),
                jax.ShapeDtypeStruct((nd, slots, 2, rows, cols), jnp.float32),
                jax.ShapeDtypeStruct((-(-size * nd // (31 // digits)), 128), jnp.int32),
            ],
            in_specs=[vmem] * len(operands),
            out_specs=[vmem] * 4,
            scratch_shapes=scratch(slots, slots)[:2],
            compiler_params=params,
            cost_estimate=work(slots),
            name="early_dates",
        )(*operands)
        operands = [words, own, power, done, edge_3, inner_3, near_b, far_b, band]
        return pl.pallas_call(
            functools.partial(kernel, ([nd], [nd], [nd]), nd, slots, "last", n_rows, digits),
            out_shape=out_shape,
            in_specs=[vmem] * len(operands),
            out_specs=hbm,
            scratch_shapes=scratch(nd, nd) + [pltpu.SemaphoreType.DMA((size * nd,))],
            compiler_params=params,
            cost_estimate=work(nd),
            name="last_dates",
        )(*operands)

    gathered = lax.all_gather(stack_data, "date", axis=0, tiled=True)
    all_edge, all_inner = cut(gathered)
    operands = [edge, all_edge, inner, all_inner, rim_near(edge), rim_near(all_edge), rim_far(edge), rim_far(all_edge)]
    slots = next(n for n in (8, 4, 2, 1) if (size * nd) % n == 0)

    def spec(array, chunk):
        if chunk:
            return pl.BlockSpec((slots,) + array.shape[1:], lambda g: (g, 0, 0, 0))
        return pl.BlockSpec(array.shape, lambda g: (0,) * array.ndim)

    return pl.pallas_call(
        functools.partial(kernel, ([nd, slots],) * 3, nd, 0, "all", n_rows, digits),
        grid=(size * nd // slots,),
        out_shape=out_shape,
        in_specs=[vmem] + [spec(a, n % 2) for n, a in enumerate(operands)] + [spec(band, 0)],
        out_specs=hbm,
        scratch_shapes=scratch(nd + slots, slots)
        + [
            pltpu.VMEM(own_shape, jnp.float32),
            pltpu.VMEM(power_shape, jnp.float32),
            pltpu.SemaphoreType.DMA((slots,)),
        ],
        compiler_params=params,
        name="all_dates",
    )(listed, *operands, band)


def solution(mesh):
    placed = (P(("grp", "date"), None, "row", None), P())
    return jax.shard_map(
        body,
        mesh=mesh,
        in_specs=placed,
        out_specs=P(("grp", "date"), None, None, "row", None),
        check_vma=False,
    )
```

```python
import functools

import jax
import jax.numpy as jnp
from jax import lax
from jax.experimental import pallas as pl
from jax.experimental.pallas import tpu as pltpu
from jax.sharding import PartitionSpec as P

HALF_ROWS = 4
HALF_COLS = 16
LANES = 128
epsilon = 1e-06


def split(x):
    high = x.astype(jnp.bfloat16)
    low = (x - high.astype(jnp.float32)).astype(jnp.bfloat16)
    return high, low


def row_window(f, rows):
    length = f.shape[0]
    total, width = f, 1
    while width < 2 * HALF_ROWS:
        total = total + pltpu.roll(total, length - width, 0)
        width *= 2
    return total[:rows] + f[2 * HALF_ROWS:]


def kernel(counts, nd, own, stage, n_rows, digits, *refs):
    def take(n):
        nonlocal refs
        head, refs = refs[:n], refs[n:]
        return head

    each = 31 // digits
    (plan_ref,) = take(1)
    own_ref, own_power, done = take(3) if stage == "last" else (None,) * 3
    edges, inners, rim_c, rim_x = (take(len(counts[n])) for n in (0, 0, 1, 2))
    (band_ref,) = take(1)
    if stage == "early":
        own_ref, own_power, buf, words_ref, ext, res = refs
    elif stage == "last":
        out_ref, ext, res, buf, sems = refs
    else:
        out_ref, ext, res, buf, own_ref, own_power, sems = refs
    half = HALF_ROWS
    rows = inners[0].shape[2] + 2 * half
    first = nd if stage == "all" else 0
    slots = sum(counts[0]) - first
    row = lax.axis_index("row")
    odd = row % 2 == 1
    copies = []

    if stage == "early":
        listed = plan_ref[...]
        slot_of = ((listed // nd) ^ lax.axis_index("date")) * nd + listed % nd
        lane = lax.broadcasted_iota(jnp.int32, listed.shape, 1)
        for w in range(words_ref.shape[0]):
            word = jnp.where(slot_of // each == w, lane << (slot_of % each * digits), 0)
            words_ref[w:w + 1] = jnp.broadcast_to(jnp.sum(word, axis=1, keepdims=True), (1, words_ref.shape[1]))
    elif stage == "last":
        words = [jnp.max(plan_ref[w:w + 1, :1]) for w in range(plan_ref.shape[0])]

    def place(slot, date):
        if stage == "last":
            return (words[slot // each] >> (slot % each * digits)) & ((1 << digits) - 1)
        listed = plan_ref[...]
        lane = lax.broadcasted_iota(jnp.int32, listed.shape, 1)
        return jnp.sum(jnp.where(listed == date, lane, 0))

    def send(ref, slot):
        if stage == "all":
            date = pl.program_id(0) * slots + slot
        else:
            date = (lax.axis_index("date") ^ (slot // nd)) * nd + slot % nd
        k = place(slot, date)
        copy = pltpu.make_async_copy(ref, out_ref.at[:, k], sems.at[slot])
        copy.start()
        copies.append(copy)

    at = 0
    for ref, inner, count in zip(edges, inners, counts[0]):
        for d in range(count):
            to = own_ref.at[at] if stage != "last" and at < nd else ext.at[at]
            to[:, half:2 * half] = ref[d, :, half:]
            to[:, 2 * half:rows] = inner[d]
            to[:, rows:rows + half] = ref[d, :, :half]
            at += 1
    near = [r.at[d] for r, count in zip(rim_c, counts[1]) for d in range(count)]
    far = [r.at[d] for r, count in zip(rim_x, counts[2]) for d in range(count)]
    for at, (c, x) in enumerate(zip(near, far)):
        to = own_ref.at[at] if stage != "last" and at < nd else ext.at[at]
        top = jnp.where(odd, c[...], x[...])
        bottom = jnp.where(odd, x[...], c[...])
        to[:, :half] = jnp.where(row == 0, 0.0, top)
        to[:, rows + half:] = jnp.where(row == n_rows - 1, 0.0, bottom)

    band = band_ref[...]

    def columns(fields):
        high, low = zip(*(split(f) for f in fields))
        both = jnp.concatenate(high + low, axis=0)
        tiles = both.shape[1] // LANES
        height = both.shape[0] // 2
        lane = lax.broadcasted_iota(jnp.int32, (height, LANES), 1)
        parts = []
        for t in range(tiles - 1):
            out = jnp.dot(both[:, t * LANES:(t + 2) * LANES], band, preferred_element_type=jnp.float32)
            parts.append(out[:height] + out[height:])
        sums = [parts[0][:, :LANES]]
        for t in range(1, tiles - 1):
            sums.append(jnp.where(lane < LANES // 2, parts[t - 1][:, LANES:], parts[t][:, :LANES]))
        sums.append(parts[-1][:, LANES:])
        return jnp.concatenate(sums, axis=1)

    def power_of(re, im):
        return row_window(re * re + im * im, rows)

    def cross_of(mr, mi, re, im):
        return [row_window(mr * re + mi * im, rows), row_window(mi * re - mr * im, rows)]

    def scale(a, b):
        return lax.rsqrt(a * b + epsilon)

    if stage != "last":
        fields = [power_of(own_ref[d, 0], own_ref[d, 1]) for d in range(nd)]
        pairs = [(d, s) for s in range(nd) for d in range(s)] if stage == "early" else []
        for d, s in pairs:
            fields += cross_of(own_ref[d, 0], own_ref[d, 1], own_ref[s, 0], own_ref[s, 1])
        sums = columns(fields)
        for d in range(nd):
            own_power[d] = sums[d * rows:(d + 1) * rows]
        if stage == "early":
            for d in range(nd):
                power = own_power[d]
                buf[d, d, 0] = power * scale(power, power)
                buf[d, d, 1] = jnp.zeros_like(power)
            for n, (d, s) in enumerate(pairs):
                at = (nd + 2 * n) * rows
                factor = scale(own_power[d], own_power[s])
                real, imag = sums[at:at + rows] * factor, sums[at + rows:at + 2 * rows] * factor
                buf[d, s, 0], buf[d, s, 1] = real, imag
                buf[s, d, 0], buf[s, d, 1] = real, -imag

    for s in range(nd if stage == "early" else 0, slots):
        re, im = ext[first + s, 0], ext[first + s, 1]
        fields = [power_of(re, im)]
        for d in range(nd):
            fields += cross_of(own_ref[d, 0], own_ref[d, 1], re, im)
        sums = columns(fields)
        power = sums[:rows]
        for d in range(nd):
            factor = scale(own_power[d], power)
            at = (1 + 2 * d) * rows
            buf[d, s, 0] = sums[at:at + rows] * factor
            buf[d, s, 1] = sums[at + rows:at + 2 * rows] * factor
        if stage == "last" and s == 0:
            for t in range(own):
                send(done.at[:, t], t)
        if stage != "early":
            send(buf.at[:, s], own + s)
    for copy in copies:
        copy.wait()


def pairs_of(size, flip):
    return [(i, i ^ flip) for i in range(size)]


def body(stack_data, plan):
    nd, _, rows, cols = stack_data.shape
    size, n_rows = lax.axis_size("date"), lax.axis_size("row")
    half = HALF_ROWS
    odd = lax.axis_index("row") % 2 == 1

    near = [(i, i ^ 1) for i in range(n_rows) if (i ^ 1) < n_rows]
    far = [(i, (i + 1) % n_rows) for i in range(1, n_rows, 2)] if n_rows % 2 == 0 else [
        (i, i + 1) for i in range(1, n_rows - 1, 2)]
    far = far + [(j, i) for i, j in far if i != j]

    def cut(block):
        first, last = block[:, :, :half], block[:, :, rows - half:]
        return jnp.concatenate([last, first], axis=2), block[:, :, half:rows - half]

    def rim_near(edge):
        last, first = edge[:, :, :half], edge[:, :, half:]
        return lax.ppermute(jnp.where(odd, first, last), "row", near)

    def rim_far(edge):
        last, first = edge[:, :, :half], edge[:, :, half:]
        return lax.ppermute(jnp.where(odd, last, first), "row", far)

    def across(edge, flip):
        last, first = edge[:, :, :half], edge[:, :, half:]
        pairs = [((d ^ flip) * n_rows + j, d * n_rows + i) for d in range(size) for i, j in far]
        return lax.ppermute(jnp.where(odd, last, first), ("date", "row"), pairs)

    def z(array, flip):
        return lax.ppermute(array, "date", pairs_of(size, flip))

    def after(array, *others):
        return lax.optimization_barrier((array,) + others)[0]

    def after(array, *others):
        return lax.optimization_barrier((array,) + others)[0]

    def join(*blocks):
        return jnp.concatenate(blocks, axis=0)

    out_col = lax.broadcasted_iota(jnp.int32, (2 * LANES, 2 * LANES), 0)
    in_col = lax.broadcasted_iota(jnp.int32, (2 * LANES, 2 * LANES), 1)
    band = (jnp.abs(out_col - in_col) <= HALF_COLS).astype(jnp.bfloat16)
    out_shape = jax.ShapeDtypeStruct((nd, size * nd, 2, rows, cols), jnp.float32)
    own_shape = (nd, 2, rows + 2 * half, cols)
    power_shape = (nd, rows, cols)
    vmem = pl.BlockSpec(memory_space=pltpu.VMEM)
    listed = jnp.maximum(plan, 0).reshape(1, -1)
    digits = max(1, (size * nd - 1).bit_length())
    hbm = pl.BlockSpec(memory_space=pl.ANY)

    def scratch(total, slots):
        return [
            pltpu.VMEM((total, 2, rows + 2 * half, cols), jnp.float32),
            pltpu.VMEM((slots, (1 + 2 * nd) * rows, cols), jnp.float32),
            pltpu.VMEM((nd, slots, 2, rows, cols), jnp.float32),
        ]

    def work(slots):
        pairs = slots * nd * rows * cols
        return pl.CostEstimate(flops=16 * pairs * cols, bytes_accessed=16 * pairs, transcendentals=pairs)

    params = pltpu.CompilerParams(vmem_limit_bytes=32 * 2**20)
    edge, inner = cut(stack_data)
    if size == 4:
        edge_2 = z(edge, 2)
        inner_2 = z(inner, 2)
        edge_1 = z(edge, 1)
        inner_1 = z(after(inner, edge), 1)
        far_b = across(edge_2, 1)
        edge_3 = z(edge_2, 1)
        inner_3 = z(inner_2, 1)
        early = join(edge, edge_1, edge_2)
        far_a = rim_far(early)
        near_a, near_b = rim_near(early), rim_near(after(edge_3, inner_1))
        slots = 3 * nd
        operands = [listed, edge, edge_1, edge_2, inner, inner_1, inner_2, near_a, far_a, band]
        own, power, done, words = pl.pallas_call(
            functools.partial(kernel, ([nd] * 3, [slots], [slots]), nd, 0, "early", n_rows, digits),
            out_shape=[
                jax.ShapeDtypeStruct(own_shape, jnp.float32),
                jax.ShapeDtypeStruct(power_shape, jnp.float32),
                jax.ShapeDtypeStruct((nd, slots, 2, rows, cols), jnp.float32),
                jax.ShapeDtypeStruct((-(-size * nd // (31 // digits)), 128), jnp.int32),
            ],
            in_specs=[vmem] * len(operands),
            out_specs=[vmem] * 4,
            scratch_shapes=scratch(slots, slots)[:2],
            compiler_params=params,
            cost_estimate=work(slots),
            name="early_dates",
        )(*operands)
        operands = [words, own, power, done, edge_3, inner_3, near_b, far_b, band]
        return pl.pallas_call(
            functools.partial(kernel, ([nd], [nd], [nd]), nd, slots, "last", n_rows, digits),
            out_shape=out_shape,
            in_specs=[vmem] * len(operands),
            out_specs=hbm,
            scratch_shapes=scratch(nd, nd) + [pltpu.SemaphoreType.DMA((size * nd,))],
            compiler_params=params,
            cost_estimate=work(nd),
            name="last_dates",
        )(*operands)

    gathered = lax.all_gather(stack_data, "date", axis=0, tiled=True)
    all_edge, all_inner = cut(gathered)
    operands = [edge, all_edge, inner, all_inner, rim_near(edge), rim_near(all_edge), rim_far(edge), rim_far(all_edge)]
    slots = next(n for n in (8, 4, 2, 1) if (size * nd) % n == 0)

    def spec(array, chunk):
        if chunk:
            return pl.BlockSpec((slots,) + array.shape[1:], lambda g: (g, 0, 0, 0))
        return pl.BlockSpec(array.shape, lambda g: (0,) * array.ndim)

    return pl.pallas_call(
        functools.partial(kernel, ([nd, slots],) * 3, nd, 0, "all", n_rows, digits),
        grid=(size * nd // slots,),
        out_shape=out_shape,
        in_specs=[vmem] + [spec(a, n % 2) for n, a in enumerate(operands)] + [spec(band, 0)],
        out_specs=hbm,
        scratch_shapes=scratch(nd + slots, slots)
        + [
            pltpu.VMEM(own_shape, jnp.float32),
            pltpu.VMEM(power_shape, jnp.float32),
            pltpu.SemaphoreType.DMA((slots,)),
        ],
        compiler_params=params,
        name="all_dates",
    )(listed, *operands, band)


def solution(mesh):
    placed = (P(("grp", "date"), None, "row", None), P())
    return jax.shard_map(
        body,
        mesh=mesh,
        in_specs=placed,
        out_specs=P(("grp", "date"), None, None, "row", None),
        check_vma=False,
    )
```
